256 devices in a mesh: leaf: 32 (over z, y), front: 8 (over x, core).
Axes of the slice: x: 4, y: 4, z: 8, core: 2. Of those that a mesh axis runs over, the one named last changes fastest.
Arguments:
- child_u: bfloat16 [1048576, 128], P(('leaf', 'front')), may hold values from -6 to 6
- child_v: bfloat16 [1048576, 128], P(('leaf', 'front')), may hold values from -0.59765625 to 0.59765625
- sketch: bfloat16 [3, 1048576, 128], P(None, ('leaf', 'front')), may hold values from -6 to 6
- map_own: int32 [3, 1048576], P(None, ('leaf', 'front')), may hold values from 0 to 4095
- map_peer: int32 [3, 1048576], P(None, ('leaf', 'front')), may hold values from 0 to 4095
- live_rows: int32 [3, 256], P(None, ('leaf', 'front')), may hold values from 1 to 4096, 655360 in all within a row
- front_panel: bfloat16 [1048576, 128], P(('leaf', 'front')), may hold values from -6 to 6
- pivot_inverse: bfloat16 [4096, 128], P('leaf'), may hold values from -0.5 to 0.5
Outputs:
- left_out: bfloat16 [1048576, 128], P(('leaf', 'front'))
- right_out: bfloat16 [1048576, 128], P(('leaf', 'front'))
- panel_out: bfloat16 [1048576, 128], P(('leaf', 'front'))
The draws below stay inside these ranges and needn't reach their ends.
Inputs may be any that keep to these rules, and one draw needn't show every extreme that they name: `live_rows`: in each level every row of 256 counts sums to 655360, the largest being 4096 and the smallest at least 256.
All inputs are finite; a program needn't handle non-finite values. No bound on the sum of `live_rows` on one device may be relied on, other than what follows from the above.
Results may differ from the reference program's by a relative error of at most 0.01235.
Values may be sent and summed in bfloat16 or wider, within the bound.
No kernel may reach another device: no remote copies, remote signals or barrier semaphores. Data moves between devices by JAX's collectives and lax.ppermute only.
A program may use at most 64 MiB of HBM per device.

```python
import math
import jax
import jax.numpy as jnp
import numpy as np
from jax import lax

R = 128
PW = 128
LEVELS = 3
ROWS = 4096
SLOTS = 256
TOTAL_ROWS = 1048576
LIVE_SUM = 655360
PIVOT_ROWS = 4096
N_LEAF = 32
N_FRONT = 8


def touch_ends(array, key, least, high):
    index_at = [jax.random.randint(jax.random.fold_in(key, axis), (), 0, length) for axis, length in enumerate(array.shape)]
    main_axis = array.shape.index(max(array.shape))
    next_to = index_at[:main_axis] + [(index_at[main_axis] + 1) % array.shape[main_axis]] + index_at[main_axis + 1:]
    return array.at[tuple(index_at)].set(least).at[tuple(next_to)].set(high)


def steps_of(rng, shape, shards, smallest, high):
    gain, own = 1.0, jax.random.fold_in(rng, 6)
    for position, parts in shards:
        draws = jnp.exp(jax.random.uniform(jax.random.fold_in(own, position), (parts,), jnp.float32, smallest / len(shards), high / len(shards)))
        gain = gain * jnp.repeat(draws, shape[position] // parts).reshape([-1 if axis == position else 1 for axis in range(len(shape))])
    return gain


def profile(count, total, bound, skew):
    loads = [(1 << 20) // math.isqrt(grade ** skew) + 1 for grade in range(2, count + 1)]
    rest, counts = total - bound - (count - 1), [1] * (count - 1)
    while rest > 0:
        free = [i for i in range(count - 1) if counts[i] < bound]
        whole, left = sum([loads[i] for i in free]), rest
        for i in free:
            addition = min(bound - counts[i], max(1, left * loads[i] // whole), rest)
            counts[i] = counts[i] + addition
            rest = rest - addition
    return np.array([bound] + counts)


def uneven_parts(rng, amount, total, most, slope):
    if amount == 2:
        one = jax.random.randint(rng, (), max(1, total - most), min(most, total - 1) + 1)
        return jnp.stack([one, total - one])
    lengths = jnp.asarray(profile(amount, total, most, slope), jnp.int32)
    pairs = (amount - 1) // 2
    source_of, receiver = lengths[1:1 + 2 * pairs:2], lengths[2:2 + 2 * pairs:2]
    slack = jnp.minimum(source_of - 1, most - receiver)
    shifted = jax.random.randint(jax.random.fold_in(rng, 1), (pairs,), 0, 1 << 20) % (slack + 1)
    lengths = lengths.at[1:1 + 2 * pairs:2].set(source_of - shifted).at[2:2 + 2 * pairs:2].set(receiver + shifted)
    return lengths[jax.random.permutation(jax.random.fold_in(rng, 2), amount)]


def scatter_about(key, extent, width, most, pieces=(), kind=jnp.bfloat16):
    loudness = steps_of(key, extent, pieces, -0.22, 0.18) if pieces else 1.0
    entries = jax.random.normal(key, extent, jnp.float32) * width * loudness
    return jnp.minimum(jnp.maximum(entries, -most), most).astype(kind)


def setup_inputs(seed: int = 0) -> dict:
    splits = jax.random.split(jax.random.key(seed), 9)
    return {
        "child_u": scatter_about(splits[0], (TOTAL_ROWS, R), 1.0, 6.0, ((0, 256),)),
        "child_v": scatter_about(splits[1], (TOTAL_ROWS, R), 0.1, 0.59765625, ((0, 256),)),
        "sketch": scatter_about(splits[2], (LEVELS, TOTAL_ROWS, R), 1.0, 6.0, ((1, 256),)),
        "map_own": touch_ends(jax.random.randint(splits[3], (LEVELS, TOTAL_ROWS), 0, ROWS), jax.random.fold_in(splits[3], 1), 0, ROWS - 1).astype(jnp.int32),
        "map_peer": touch_ends(jax.random.randint(splits[4], (LEVELS, TOTAL_ROWS), 0, ROWS), jax.random.fold_in(splits[4], 1), 0, ROWS - 1).astype(jnp.int32),
        "live_rows": jax.vmap(lambda own: uneven_parts(own, SLOTS, LIVE_SUM, ROWS, 0))(jax.random.split(splits[5], LEVELS)).reshape((LEVELS, SLOTS)).astype(jnp.int32),
        "front_panel": scatter_about(splits[6], (TOTAL_ROWS, PW), 1.0, 6.0, ((0, 256),)),
        "pivot_inverse": scatter_about(splits[7], (PIVOT_ROWS, PW), PW ** -0.5, 0.5, ((0, 32),)),
    }


HIGHEST_PREC = lax.Precision.HIGHEST

def pick_rows(source, index):
    return jnp.take_along_axis(source, index[..., None], axis=2)

def reference(child_u, child_v, sketch, map_own, map_peer, live_rows, front_panel, pivot_inverse):
    left = child_u.reshape(N_LEAF, N_FRONT, ROWS, R)
    right = child_v.reshape(N_LEAF, N_FRONT, ROWS, R)
    row_index = jnp.arange(ROWS, dtype=jnp.int32)
    for tree_level in range(LEVELS):
        group_size = 2 ** (tree_level + 1)
        peer_index = np.arange(N_LEAF) ^ 2 ** tree_level
        map_self = map_own[tree_level].reshape(N_LEAF, N_FRONT, ROWS)
        map_other = map_peer[tree_level].reshape(N_LEAF, N_FRONT, ROWS)
        live = live_rows[tree_level].reshape(N_LEAF, N_FRONT)
        row_keep = (row_index[None, None, :] < live[:, :, None])[..., None]
        left_cat = jnp.concatenate([pick_rows(left, map_self), pick_rows(left[peer_index], map_other)], -1)
        right_cat = jnp.concatenate([pick_rows(right, map_self), pick_rows(right[peer_index], map_other)], -1)
        left_cat = jnp.where(row_keep, left_cat, 0).astype(jnp.bfloat16)
        right_cat = jnp.where(row_keep, right_cat, 0).astype(jnp.bfloat16)
        groups = N_LEAF // group_size
        span = group_size * N_FRONT * ROWS
        left_g = left_cat.reshape(groups, span, 2 * R).astype(jnp.float32)
        right_g = right_cat.reshape(groups, span, 2 * R).astype(jnp.float32)
        omega = sketch[tree_level].reshape(groups, span, R).astype(jnp.float32)
        sketch_b = jnp.einsum('gnr,gns->grs', right_g, omega, precision=HIGHEST_PREC)
        basis = jnp.einsum('gnr,grs->gns', left_g, sketch_b, precision=HIGHEST_PREC)
        gram = jnp.einsum('gnr,gns->grs', basis, basis, precision=HIGHEST_PREC)
        lower = jnp.linalg.cholesky(gram)
        ortho = lax.linalg.triangular_solve(lower, basis, left_side=False, lower=True, transpose_a=True)
        project = jnp.einsum('gnr,gns->grs', left_g, ortho, precision=HIGHEST_PREC)
        norm_scale = float(np.sqrt(span))
        left = (ortho * norm_scale).astype(jnp.bfloat16).reshape(N_LEAF, N_FRONT, ROWS, R)
        right_new = jnp.einsum('gnr,grs->gns', right_g, project, precision=HIGHEST_PREC)
        right = (right_new / norm_scale).astype(jnp.bfloat16).reshape(N_LEAF, N_FRONT, ROWS, R)
    right_piv = right[:, 0, :PW, :].astype(jnp.float32)
    panel_f = front_panel.reshape(N_LEAF, N_FRONT, ROWS, PW).astype(jnp.float32)
    updated = panel_f - jnp.einsum('lfnr,lpr->lfnp', left.astype(jnp.float32), right_piv, precision=HIGHEST_PREC)
    inverse_f = pivot_inverse.reshape(N_LEAF, PW, PW).astype(jnp.float32)
    panel_out = jnp.einsum('lfnp,lpq->lfnq', updated, inverse_f, precision=HIGHEST_PREC).astype(jnp.bfloat16)
    return (left.reshape(TOTAL_ROWS, R), right.reshape(TOTAL_ROWS, R), panel_out.reshape(TOTAL_ROWS, PW))
```

```python
import functools
import math

import jax
import jax.numpy as jnp
from jax import lax
from jax.experimental import pallas as pl
from jax.experimental.pallas import tpu as pltpu
from jax.sharding import PartitionSpec as P

F32, BF16 = jnp.float32, jnp.bfloat16
HIGHEST = lax.Precision.HIGHEST
NT = (((1,), (1,)), ((), ()))
TN = (((0,), (0,)), ((), ()))
VMEM = pl.BlockSpec(memory_space=pltpu.VMEM)
SMEM = pl.BlockSpec(memory_space=pltpu.SMEM)
R = 128
UNROLL = 32


def swap(block, axis, mask):
    route = [(i, i ^ mask) for i in range(lax.axis_size(axis))]
    return lax.ppermute(block, axis, route)


def gather_body(level, index, live, a, b, oa, ob, src, dst):
    rows = a.shape[0]
    src[pl.ds(0, rows, 2), :] = a[...].astype(F32)
    src[pl.ds(1, rows, 2), :] = b[...].astype(F32)

    def step(g, carry):
        for k in range(UNROLL):
            j = g * UNROLL + k
            i = index[level, j]
            dst[pl.ds(pl.multiple_of(2 * j, 2), 2), :] = src[pl.ds(pl.multiple_of(2 * i, 2), 2), :]
        return carry

    lax.fori_loop(0, rows // UNROLL, step, 0)
    keep = lax.broadcasted_iota(jnp.int32, (rows, R), 0) < live[level, 0]
    oa[...] = jnp.where(keep, dst[pl.ds(0, rows, 2), :], 0).astype(BF16)
    ob[...] = jnp.where(keep, dst[pl.ds(1, rows, 2), :], 0).astype(BF16)


def gather_pair(level, index, live, a, b):
    rows = a.shape[0]
    return pl.pallas_call(
        functools.partial(gather_body, level),
        out_shape=[jax.ShapeDtypeStruct((rows, R), BF16)] * 2,
        in_specs=[SMEM, SMEM, VMEM, VMEM],
        out_specs=[VMEM, VMEM],
        scratch_shapes=[pltpu.VMEM((2 * rows, R), F32)] * 2,
        cost_estimate=pl.CostEstimate(flops=1 << 24, bytes_accessed=16 << 20, transcendentals=0),
        compiler_params=pltpu.CompilerParams(vmem_limit_bytes=32 << 20),
        name="gather_pair",
    )(index, live, a, b)


def sums_body(la, lb, ra, rb, sk, out):
    rows, chunk = la.shape[0], 1024
    total = None
    for k in range(rows // chunk):
        at = pl.ds(k * chunk, chunk)
        left = jnp.concatenate([la[at, :], lb[at, :]], 1)
        right = jnp.concatenate([ra[at, :], rb[at, :]], 1)
        bt = lax.dot_general(sk[at, :], right, TN, preferred_element_type=F32)
        gr = lax.dot_general(left, left, TN, preferred_element_type=F32)
        total = (bt, gr) if total is None else (total[0] + bt, total[1] + gr)
    bt, gr = total
    out[0:R, :] = bt[:, :R]
    out[R : 2 * R, :] = bt[:, R:]
    out[2 * R : 3 * R, :] = gr[:R, :R]
    out[3 * R : 4 * R, :] = gr[:R, R:]
    out[4 * R : 5 * R, :] = gr[R:, R:]


def local_sums(la, lb, ra, rb, sk):
    return pl.pallas_call(
        sums_body,
        out_shape=jax.ShapeDtypeStruct((5 * R, R), F32),
        in_specs=[VMEM] * 5,
        out_specs=VMEM,
        name="local_sums",
    )(la, lb, ra, rb, sk)


def group_sum(part, level):
    half = part.shape[0] // 2
    core = lax.axis_index("front") % 2
    mine = lax.dynamic_slice_in_dim(part, core * half, half, 0)
    give = lax.dynamic_slice_in_dim(part, (1 - core) * half, half, 0)
    mine = mine + swap(give, "front", 1)
    for axis, mask in [("front", 2), ("front", 4)] + [("leaf", 1 << b) for b in range(level + 1)]:
        mine = mine + swap(mine, axis, mask)
    return mine, swap(mine, "front", 1)


def factor_body(scale, core, mine, other, z_out, p_out, tot, m):
    half = mine.shape[0]
    c = core[0]
    tot[pl.ds(pl.multiple_of(c * half, 8), half), :] = mine[...]
    tot[pl.ds(pl.multiple_of((1 - c) * half, 8), half), :] = other[...]
    bt = jnp.concatenate([tot[0:R, :], tot[R : 2 * R, :]], 1)
    g12 = tot[3 * R : 4 * R, :]
    g = jnp.concatenate(
        [
            jnp.concatenate([tot[2 * R : 3 * R, :], g12], 1),
            jnp.concatenate([g12.T, tot[4 * R : 5 * R, :]], 1),
        ],
        0,
    )
    bg = jnp.dot(bt, g, precision=HIGHEST, preferred_element_type=F32)
    m[:, 0:R] = lax.dot_general(bg, bt, NT, precision=HIGHEST, preferred_element_type=F32)
    m[:, R : 3 * R] = bt
    m[:, 3 * R : 5 * R] = bg
    panel, parts = 32, 5
    sub = lax.broadcasted_iota(jnp.int32, (8, R), 0)
    tiles = panel // 8

    def spread(x):
        return jnp.broadcast_to(x, (8, R))

    for top in range(0, R, panel):
        w = [
            [m[top + 8 * t : top + 8 * t + 8, R * q : R * q + R] for q in range(parts)]
            for t in range(tiles)
        ]
        for b in range(tiles):
            at = top + 8 * b
            v = {
                (i, t): spread(w[t][0][:, at + i : at + i + 1])
                for i in range(8)
                for t in range(b, tiles)
            }
            for i in range(8):
                inv = lax.rsqrt(spread(v[i, b][i : i + 1, :]))
                row = [spread(w[b][q][i : i + 1, :]) * inv for q in range(parts)]
                ahead = {j: spread(v[j, b][i : i + 1, :]) * inv for j in range(i + 1, 8)}
                for t in range(b, tiles):
                    mult = v[i, t] * inv
                    if t == b:
                        mult = jnp.where(sub > i, mult, 0.0)
                    for q in range(parts):
                        new = w[t][q] - mult * row[q]
                        w[t][q] = jnp.where(sub == i, row[q], new) if t == b else new
                    for j in range(i + 1, 8):
                        v[j, t] = v[j, t] - mult * ahead[j]
        u = jnp.concatenate([jnp.concatenate(r, 1) for r in w], 0)
        z_out[top : top + panel, :] = u[:, R : 3 * R] * scale
        p_out[top : top + panel, :] = u[:, 3 * R : 5 * R] * (1.0 / scale)
        if top + panel < R:
            update = lax.dot_general(u[:, 0:R], u, TN, precision=HIGHEST, preferred_element_type=F32)
            m[top + panel :, :] = m[top + panel :, :] - update[top + panel :, :]


def factor(core, mine, other, scale):
    return pl.pallas_call(
        functools.partial(factor_body, scale),
        out_shape=[jax.ShapeDtypeStruct((R, 2 * R), F32)] * 2,
        in_specs=[SMEM, VMEM, VMEM],
        out_specs=[VMEM, VMEM],
        scratch_shapes=[pltpu.VMEM((5 * R, R), F32), pltpu.VMEM((R, 5 * R), F32)],
        name="factor",
    )(core, mine, other)


def split(w):
    high = w.astype(BF16)
    return jnp.concatenate([high, (w - high.astype(F32)).astype(BF16)], 0)


def times(a, b, w):
    d = lax.dot_general(jnp.concatenate([a, b], 1), w, NT, preferred_element_type=F32)
    return (d[:, :R] + d[:, R:]).astype(BF16)


def apply_body(la, lb, ra, rb, z, p, left, right):
    rows, chunk = la.shape[0], 512
    zz, pp = split(z[...]), split(p[...])
    for k in range(rows // chunk):
        at = pl.ds(k * chunk, chunk)
        left[at, :] = times(la[at, :], lb[at, :], zz)
        right[at, :] = times(ra[at, :], rb[at, :], pp)


def apply(la, lb, ra, rb, z, p):
    rows = la.shape[0]
    return pl.pallas_call(
        apply_body,
        out_shape=[jax.ShapeDtypeStruct((rows, R), BF16)] * 2,
        in_specs=[VMEM] * 6,
        out_specs=[VMEM] * 2,
        name="apply",
    )(la, lb, ra, rb, z, p)


def finish_body(la, lb, ra, rb, z, p, top, front, pivot, left, right, panel):
    rows, chunk = la.shape[0], 512
    zz, pp = split(z[...]), split(p[...])
    right_piv = times(top[:, :R], top[:, R:], pp)
    inverse = jnp.concatenate([pivot[...], pivot[...]], 0)
    for k in range(rows // chunk):
        at = pl.ds(k * chunk, chunk)
        new = times(la[at, :], lb[at, :], zz)
        left[at, :] = new
        right[at, :] = times(ra[at, :], rb[at, :], pp)
        updated = front[at, :].astype(F32) - lax.dot_general(
            new, right_piv, NT, preferred_element_type=F32
        )
        high = updated.astype(BF16)
        low = (updated - high.astype(F32)).astype(BF16)
        panel[at, :] = jnp.dot(
            jnp.concatenate([high, low], 1), inverse, preferred_element_type=F32
        ).astype(BF16)


def finish(la, lb, ra, rb, z, p, top, front, pivot):
    rows = la.shape[0]
    return pl.pallas_call(
        finish_body,
        out_shape=[jax.ShapeDtypeStruct((rows, R), BF16)] * 3,
        in_specs=[VMEM] * 9,
        out_specs=[VMEM] * 3,
        compiler_params=pltpu.CompilerParams(vmem_limit_bytes=32 << 20),
        name="finish",
    )(la, lb, ra, rb, z, p, top, front, pivot)


def from_first(block):
    me = lax.axis_index("front")
    for have, mask in (((0,), 2), ((0, 2), 4), ((0, 2, 4, 6), 1)):
        came = lax.ppermute(block, "front", [(i, i + mask) for i in have])
        takes = functools.reduce(jnp.logical_or, [me == i + mask for i in have])
        block = jnp.where(takes, came, block)
    return block


def on_device(child_u, child_v, sketch, map_own, map_peer, live_rows, front_panel, pivot_inverse):
    rows, levels = child_u.shape[0], sketch.shape[0]
    fronts = lax.axis_size("front")
    core = (lax.axis_index("front") % 2).astype(jnp.int32).reshape(1)
    left, right = child_u, child_v
    for level in range(levels):
        bit = 1 << level
        peer_left, peer_right = swap(left, "leaf", bit), swap(right, "leaf", bit)
        la, ra = gather_pair(level, map_own, live_rows, left, right)
        lb, rb = gather_pair(level, map_peer, live_rows, peer_left, peer_right)
        if level == levels - 1:
            top = from_first(jnp.concatenate([ra[:R], rb[:R]], 1))
        mine, other = group_sum(local_sums(la, lb, ra, rb, sketch[level]), level)
        z, p = factor(core, mine, other, math.sqrt(2 * bit * fronts * rows))
        if level < levels - 1:
            left, right = apply(la, lb, ra, rb, z, p)
    return finish(la, lb, ra, rb, z, p, top, front_panel, pivot_inverse)


def solution(mesh):
    rows = P(("leaf", "front"), None)
    placed = (
        rows,
        rows,
        P(None, ("leaf", "front"), None),
        P(None, ("leaf", "front")),
        P(None, ("leaf", "front")),
        P(None, ("leaf", "front")),
        rows,
        P("leaf", None),
    )
    return jax.shard_map(
        on_device, mesh=mesh, in_specs=placed, out_specs=(rows, rows, rows), check_vma=False
    )
```

```python
import functools
import math

import jax
import jax.numpy as jnp
from jax import lax
from jax.experimental import pallas as pl
from jax.experimental.pallas import tpu as pltpu
from jax.sharding import PartitionSpec as P

F32, BF16 = jnp.float32, jnp.bfloat16
HIGHEST = lax.Precision.HIGHEST
NT = (((1,), (1,)), ((), ()))
TN = (((0,), (0,)), ((), ()))
VMEM = pl.BlockSpec(memory_space=pltpu.VMEM)
SMEM = pl.BlockSpec(memory_space=pltpu.SMEM)
R = 128
UNROLL = 32
BRIEF = pl.CostEstimate(flops=1, bytes_accessed=1, transcendentals=0)
PARAMS = pltpu.CompilerParams(vmem_limit_bytes=48 << 20)


def swap(block, axis, mask):
    route = [(i, i ^ mask) for i in range(lax.axis_size(axis))]
    return lax.ppermute(block, axis, route)


def pick_rows(index, src, dst, outs, width, skip=0):
    rows, count = outs[0].shape[0], len(outs)

    def step(g, carry):
        for k in range(UNROLL):
            j = g * UNROLL + k
            i = index[j]
            dst[pl.ds(pl.multiple_of(count * j, count), count), :] = src[
                pl.ds(pl.multiple_of(width * i, width) + skip, count), :
            ]
        return carry

    lax.fori_loop(0, rows // UNROLL, step, 0)
    for w in range(count):
        outs[w][...] = dst[pl.ds(w, rows, count), :].astype(BF16)


def gather_body(width, index, *refs):
    ins, outs, src, dst = refs[:width], refs[width : 2 * width], refs[-2], refs[-1]
    rows = ins[0].shape[0]
    for w in range(width):
        src[pl.ds(w, rows, width), :] = ins[w][...].astype(F32)
    src[width * rows :, :] = jnp.zeros((8, R), F32)
    pick_rows(index, src, dst, outs, width)


def gather_space(width, rows):
    return [pltpu.VMEM((width * rows + 8, R), F32), pltpu.VMEM((width * rows, R), F32)]


def gather(index, *arrays):
    rows, width = arrays[0].shape[0], len(arrays)
    return pl.pallas_call(
        functools.partial(gather_body, width),
        out_shape=[jax.ShapeDtypeStruct((rows, R), BF16)] * width,
        in_specs=[SMEM] + [VMEM] * width,
        out_specs=[VMEM] * width,
        scratch_shapes=gather_space(width, rows),
        cost_estimate=BRIEF,
        compiler_params=PARAMS,
        name="gather",
    )(index, *arrays)


def sums_into(pairs, ins, tot):
    rows, chunk = ins[0].shape[0], 1024
    totals = [None] * len(pairs)
    for k in range(rows // chunk):
        at = pl.ds(k * chunk, chunk)
        for n, (x, ys) in enumerate(pairs):
            y = jnp.concatenate([ins[i][at, :] for i in ys], 1) if len(ys) > 1 else ins[ys[0]][at, :]
            d = lax.dot_general(ins[x][at, :], y, TN, preferred_element_type=F32)
            totals[n] = d if totals[n] is None else totals[n] + d
    row = 0
    for d, (x, ys) in zip(totals, pairs):
        for n in range(len(ys)):
            tot[row : row + R, :] = d[:, n * R : n * R + R]
            row += R
    return row // 2


def sums_body(pairs, count, place, *refs):
    ins, (mine, give, tot) = refs[:count], refs[-3:]
    half = sums_into(pairs, ins, tot)
    c = place[0]
    mine[...] = tot[pl.ds(pl.multiple_of(c * half, 8), half), :]
    give[...] = tot[pl.ds(pl.multiple_of((1 - c) * half, 8), half), :]


def local_sums(place, pairs, arrays, after=()):
    blocks = sum(len(ys) for _, ys in pairs)
    half = blocks * R // 2
    return pl.pallas_call(
        functools.partial(sums_body, pairs, len(arrays)),
        out_shape=[jax.ShapeDtypeStruct((half, R), F32)] * 2,
        in_specs=[SMEM] + [VMEM] * len(arrays) + [pl.BlockSpec(memory_space=pl.ANY)] * len(after),
        out_specs=[VMEM, VMEM],
        scratch_shapes=[pltpu.VMEM((blocks * R, R), F32)],
        cost_estimate=BRIEF,
        compiler_params=PARAMS,
        name="local_sums",
    )(place, *arrays, *after)


def over_core(parts):
    mine, give = parts
    return mine + swap(give, "front", 1)


def over(block, axis, mask):
    return block + swap(block, axis, mask)


def add_body(a, b, *refs):
    refs[-1][...] = a[...] + b[...]


def add(a, b, after):
    return pl.pallas_call(
        add_body,
        out_shape=jax.ShapeDtypeStruct(a.shape, F32),
        in_specs=[VMEM] * 2 + [pl.BlockSpec(memory_space=pl.ANY)] * len(after),
        out_specs=VMEM,
        cost_estimate=BRIEF,
        name="add",
    )(a, b, *after)


def factor_into(scale, order, place, early, early_o, late, late_o, z_out, p_out, tot, m):
    c = place[0]
    base = 0
    for mine, other in ((early, early_o), (late, late_o)):
        half = mine.shape[0]
        tot[pl.ds(pl.multiple_of(base + c * half, 8), half), :] = mine[...]
        tot[pl.ds(pl.multiple_of(base + (1 - c) * half, 8), half), :] = other[...]
        base += 2 * half
    b1, b2, g11, g12, g22 = (tot[R * order.index(n) : R * order.index(n) + R, :] for n in range(5))
    bt = jnp.concatenate([b1, b2], 1)
    g = jnp.concatenate([jnp.concatenate([g11, g12], 1), jnp.concatenate([g12.T, g22], 1)], 0)
    bg = jnp.dot(bt, g, precision=HIGHEST, preferred_element_type=F32)
    m[:, 0:R] = lax.dot_general(bg, bt, NT, precision=HIGHEST, preferred_element_type=F32)
    m[:, R : 3 * R] = bt
    m[:, 3 * R : 5 * R] = bg
    panel, parts = 32, 5
    sub = lax.broadcasted_iota(jnp.int32, (8, R), 0)
    tiles = panel // 8

    def spread(x):
        return jnp.broadcast_to(x, (8, R))

    for top in range(0, R, panel):
        w = [
            [m[top + 8 * t : top + 8 * t + 8, R * q : R * q + R] for q in range(parts)]
            for t in range(tiles)
        ]
        for b in range(tiles):
            at = top + 8 * b
            v = {
                (i, t): spread(w[t][0][:, at + i : at + i + 1])
                for i in range(8)
                for t in range(b, tiles)
            }
            for i in range(8):
                inv = lax.rsqrt(spread(v[i, b][i : i + 1, :]))
                row = [spread(w[b][q][i : i + 1, :]) * inv for q in range(parts)]
                ahead = {j: spread(v[j, b][i : i + 1, :]) * inv for j in range(i + 1, 8)}
                for t in range(b, tiles):
                    mult = v[i, t] * inv
                    if t == b:
                        mult = jnp.where(sub > i, mult, 0.0)
                    for q in range(parts):
                        new = w[t][q] - mult * row[q]
                        w[t][q] = jnp.where(sub == i, row[q], new) if t == b else new
                    for j in range(i + 1, 8):
                        v[j, t] = v[j, t] - mult * ahead[j]
        u = jnp.concatenate([jnp.concatenate(r, 1) for r in w], 0)
        z_out[top : top + panel, :] = u[:, R : 3 * R] * scale
        p_out[top : top + panel, :] = u[:, 3 * R : 5 * R] * (1.0 / scale)
        if top + panel < R:
            update = lax.dot_general(u[:, 0:R], u, TN, precision=HIGHEST, preferred_element_type=F32)
            m[top + panel :, :] = m[top + panel :, :] - update[top + panel :, :]


FACTOR_SPACE = [
    pltpu.VMEM((R, 2 * R), F32),
    pltpu.VMEM((R, 2 * R), F32),
    pltpu.VMEM((5 * R, R), F32),
    pltpu.VMEM((R, 5 * R), F32),
]


def split(w):
    high = w.astype(BF16)
    return jnp.concatenate([high, (w - high.astype(F32)).astype(BF16)], 0)


def times(a, b, w):
    d = lax.dot_general(jnp.concatenate([a, b], 1), w, NT, preferred_element_type=F32)
    return (d[:, :R] + d[:, R:]).astype(BF16)


def left_body(how, place, index, *refs):
    sums, (la, lb, left, lq, p_out, src, dst), space = refs[:4], refs[4:11], refs[11:]
    rows, chunk = la.shape[0], 512
    z, p = space[:2]
    factor_into(*how, place, *sums, *space)
    p_out[...] = p[...]
    zz = split(z[...])
    for k in range(rows // chunk):
        at = pl.ds(k * chunk, chunk)
        new = times(la[at, :], lb[at, :], zz)
        left[at, :] = new
        src[at, :] = new.astype(F32)
    src[rows:, :] = jnp.zeros((8, R), F32)
    pick_rows(index, src, dst, (lq,), 1)


def new_left(how, place, index, sums, la, lb):
    rows = la.shape[0]
    return pl.pallas_call(
        functools.partial(left_body, how),
        out_shape=[jax.ShapeDtypeStruct((rows, R), BF16)] * 2
        + [jax.ShapeDtypeStruct((R, 2 * R), F32)],
        in_specs=[SMEM] * 2 + [VMEM] * 6,
        out_specs=[VMEM] * 3,
        scratch_shapes=gather_space(1, rows) + FACTOR_SPACE,
        cost_estimate=BRIEF,
        compiler_params=PARAMS,
        name="new_left",
    )(place, index, *sums, la, lb)


def right_body(top, place, own, asked, left, lq, p, ra, rb, sk, sk_o, *refs):
    rows, chunk = ra.shape[0], 512
    la_out, ra_out, rq, mine, give, src, dst, tot = refs
    pp = split(p[...])
    for k in range(rows // chunk):
        at = pl.ds(k * chunk, chunk)
        new = times(ra[at, :], rb[at, :], pp)
        src[pl.ds(2 * k * chunk, chunk, 2), :] = left[at, :].astype(F32)
        src[pl.ds(2 * k * chunk + 1, chunk, 2), :] = new.astype(F32)
    src[2 * rows :, :] = jnp.zeros((8, R), F32)
    pick_rows(own, src, dst, (la_out, ra_out), 2)
    pick_rows(asked, src, dst, (rq,), 2, 1)
    half = sums_into(
        ((0, (1,)), (2, (3,)), (4, (4,)), (5, (5,))), (sk, ra_out, sk_o, rq, la_out, lq), tot
    )
    c = place[0]
    mine[0:half, :] = tot[pl.ds(pl.multiple_of(c * half, 8), half), :]
    give[0:half, :] = tot[pl.ds(pl.multiple_of((1 - c) * half, 8), half), :]
    if top:
        for out, core in ((mine, c), (give, 1 - c)):
            rows_of = jnp.where(core == 0, ra_out[:R, :].astype(F32), rq[:R, :].astype(F32))
            out[half:, :] = jnp.where(place[1] == 1, rows_of, 0.0)


def new_right(top, place, own, asked, left, lq, p, ra, rb, sk, sk_o):
    rows = ra.shape[0]
    half = 2 * R + (R if top else 0)
    return pl.pallas_call(
        functools.partial(right_body, top),
        out_shape=[jax.ShapeDtypeStruct((rows, R), BF16)] * 3
        + [jax.ShapeDtypeStruct((half, R), F32)] * 2,
        in_specs=[SMEM] * 3 + [VMEM] * 7,
        out_specs=[VMEM] * 5,
        scratch_shapes=gather_space(2, rows) + [pltpu.VMEM((4 * R, R), F32)],
        cost_estimate=BRIEF,
        compiler_params=PARAMS,
        name="new_right",
    )(place, own, asked, left, lq, p, ra, rb, sk, sk_o)


def finish_body(how, place, *refs):
    sums, (la, lb, ra, rb, top, front, pivot), refs = refs[:4], refs[4:11], refs[11:]
    (left, right, panel), space = refs[:3], refs[3:]
    rows, chunk = la.shape[0], 512
    z, p = space[:2]
    factor_into(*how, place, *sums, *space)
    zz, pp = split(z[...]), split(p[...])
    right_piv = times(top[:, :R], top[:, R:], pp)
    inverse = jnp.concatenate([pivot[...], pivot[...]], 0)
    for k in range(rows // chunk):
        at = pl.ds(k * chunk, chunk)
        new = times(la[at, :], lb[at, :], zz)
        left[at, :] = new
        right[at, :] = times(ra[at, :], rb[at, :], pp)
        updated = front[at, :].astype(F32) - lax.dot_general(
            new, right_piv, NT, preferred_element_type=F32
        )
        high = updated.astype(BF16)
        low = (updated - high.astype(F32)).astype(BF16)
        panel[at, :] = jnp.dot(
            jnp.concatenate([high, low], 1), inverse, preferred_element_type=F32
        ).astype(BF16)


def finish(how, place, sums, cats, top, front, pivot):
    rows = front.shape[0]
    return pl.pallas_call(
        functools.partial(finish_body, how),
        out_shape=[jax.ShapeDtypeStruct((rows, R), BF16)] * 3,
        in_specs=[SMEM] + [VMEM] * 11,
        out_specs=[VMEM] * 3,
        scratch_shapes=FACTOR_SPACE,
        cost_estimate=BRIEF,
        compiler_params=PARAMS,
        name="finish",
    )(place, *sums, *cats, top, front, pivot)


def tied(array, *others):
    return lax.optimization_barrier((array, *others))[0]


def on_device(child_u, child_v, sketch, map_own, map_peer, live_rows, front_panel, pivot_inverse):
    rows, levels = child_u.shape[0], sketch.shape[0]
    fronts, front = lax.axis_size("front"), lax.axis_index("front")
    core = front % 2
    place = jnp.stack([core, front == 0]).astype(jnp.int32)
    dead = jnp.arange(rows, dtype=jnp.int32)[None, :] >= live_rows
    own = jnp.where(dead, rows, map_own)
    peer = jnp.where(dead, rows, map_peer)
    left_o = swap(child_u, "leaf", 1)
    asked = [swap(peer[n], "leaf", 1 << n) for n in range(levels)]
    sketch_o = [None, None] + [swap(sketch[n], "leaf", 1 << n) for n in range(2, levels)]
    (rq,) = gather(asked[0], child_v)
    la, ra = gather(own[0], child_u, child_v)
    rb = swap(rq, "leaf", 1)
    (lb,) = gather(peer[0], left_o)
    early = over_core(local_sums(place, ((0, (0, 1)), (1, (1,))), (la, lb), asked[2:]))
    early = over(early, "front", 2)
    held = [early, *asked[1:2], *sketch_o[2:]]
    late = over_core(local_sums(place, ((0, (1, 2)),), (sketch[0], ra, rb), held))
    early = over(early, "front", 4)
    both = over(jnp.concatenate([early, late], 0), "leaf", 1)
    cut = early.shape[0]
    sketch_o[1] = swap(tied(sketch[1], asked[1], both), "leaf", 2)
    order = (2, 3, 4, 0, 1)
    for level in range(1, levels):
        bit, last = 1 << level, level == levels - 1
        early, late = both[:cut], over(over(both[cut:], "front", 2), "front", 4)
        sums = (early, swap(early, "front", 1), late, swap(late, "front", 1))
        how = (math.sqrt(bit * fronts * rows), order)
        left, lq, p = new_left(how, place, asked[level], sums, la, lb)
        lb = swap(lq, "leaf", bit)
        la, ra, rq, mine, give = new_right(
            last, place, own[level], asked[level], left, lq, p, ra, rb, sketch[level], sketch_o[level]
        )
        early = over(over_core((mine, give)), "front", 2)
        late = over_core(local_sums(place, ((0, (1,)),), (la, lb), (early,)))
        early = over(early, "front", 4)
        cut, order = 2 * R, (0, 1, 2, 4, 3)
        if not last:
            both = jnp.concatenate([early, late], 0)
            for b in range(level + 1):
                both = over(both, "leaf", 1 << b)
            rb = swap(tied(rq, both), "leaf", bit)
    rb = swap(tied(rq, lb), "leaf", bit)
    top = early[cut:].astype(BF16)
    top = jnp.where(core == 0, top, swap(top, "leaf", bit))
    other = swap(top, "front", 1)
    top = jnp.concatenate([jnp.where(core == 0, top, other), jnp.where(core == 0, other, top)], 1)
    late = over(over(late, "front", 2), "front", 4)
    both = jnp.concatenate([early[:cut], late], 0)
    for b in range(levels - 2):
        both = over(both, "leaf", 1 << b)
    both = add(both, swap(both, "leaf", bit >> 1), (rb,))
    both = over(both, "leaf", bit)
    other = swap(both, "front", 1)
    sums = (both[:cut], other[:cut], both[cut:], other[cut:])
    how = (math.sqrt(2 * bit * fronts * rows), order)
    return finish(how, place, sums, (la, lb, ra, rb), top, front_panel, pivot_inverse)


def solution(mesh):
    rows = P(("leaf", "front"), None)
    placed = (
        rows,
        rows,
        P(None, ("leaf", "front"), None),
        P(None, ("leaf", "front")),
        P(None, ("leaf", "front")),
        P(None, ("leaf", "front")),
        rows,
        P("leaf", None),
    )
    return jax.shard_map(
        on_device, mesh=mesh, in_specs=placed, out_specs=(rows, rows, rows), check_vma=False
    )
```

```python
import functools
import math

import jax
import jax.numpy as jnp
from jax import lax
from jax.experimental import pallas as pl
from jax.experimental.pallas import tpu as pltpu
from jax.sharding import PartitionSpec as P

F32, BF16 = jnp.float32, jnp.bfloat16
HIGHEST = lax.Precision.HIGHEST
NT = (((1,), (1,)), ((), ()))
TN = (((0,), (0,)), ((), ()))
VMEM = pl.BlockSpec(memory_space=pltpu.VMEM)
SMEM = pl.BlockSpec(memory_space=pltpu.SMEM)
ANY = pl.BlockSpec(memory_space=pl.ANY)
R = 128
UNROLL = 32
BRIEF = pl.CostEstimate(flops=1, bytes_accessed=1, transcendentals=0)
PARAMS = pltpu.CompilerParams(vmem_limit_bytes=24 << 20)


def swap(block, axis, mask):
    route = [(i, i ^ mask) for i in range(lax.axis_size(axis))]
    return lax.ppermute(block, axis, route)


def fetch(sources, buffers, sems):
    copies = [
        pltpu.make_async_copy(source, buffer, sems.at[n])
        for n, (source, buffer) in enumerate(zip(sources, buffers))
    ]
    for copy in copies:
        copy.start()
    return copies


def held(rows, count):
    return [pltpu.VMEM((rows, R), BF16)] * count + [pltpu.SemaphoreType.DMA((count,))]


def sweep(rows, chunk, step, times=1):
    def body(k, carry):
        for n in range(times):
            step(pl.multiple_of(k * chunk * times + n * chunk, chunk))
        return carry

    lax.fori_loop(0, rows // (chunk * times), body, 0)


def load_rows(ins, src):
    rows, width, chunk = ins[0].shape[0], len(ins), 1024

    def step(at):
        for w in range(width):
            src[pl.ds(width * at + w, chunk, width), :] = ins[w][pl.ds(at, chunk), :].astype(F32)

    sweep(rows, chunk, step)
    src[width * rows :, :] = jnp.zeros((8, R), F32)


def pick_rows(index, src, dst, outs, width, skip=0):
    rows, count = outs[0].shape[0], len(outs)

    def step(g, carry):
        for k in range(UNROLL):
            j = g * UNROLL + k
            i = index[j]
            dst[pl.ds(pl.multiple_of(count * j, count), count), :] = src[
                pl.ds(pl.multiple_of(width * i, width) + skip, count), :
            ]
        return carry

    lax.fori_loop(0, rows // UNROLL, step, 0)

    def store(at):
        for w in range(count):
            outs[w][pl.ds(at, 1024), :] = dst[pl.ds(count * at + w, 1024, count), :].astype(BF16)

    sweep(rows, 1024, store)


def gather_body(width, index, *refs):
    ins, outs, src, dst = refs[:width], refs[width : 2 * width], refs[-2], refs[-1]
    load_rows(ins, src)
    pick_rows(index, src, dst, outs, width)


def gather_space(width, rows):
    return [pltpu.VMEM((width * rows + 8, R), F32), pltpu.VMEM((width * rows, R), F32)]


def gather(index, *arrays):
    rows, width = arrays[0].shape[0], len(arrays)
    return pl.pallas_call(
        functools.partial(gather_body, width),
        out_shape=[jax.ShapeDtypeStruct((rows, R), BF16)] * width,
        in_specs=[SMEM] + [VMEM] * width,
        out_specs=[VMEM] * width,
        scratch_shapes=gather_space(width, rows),
        cost_estimate=BRIEF,
        compiler_params=PARAMS,
        name="gather",
    )(index, *arrays)


def sums_into(pairs, ins, tot):
    rows, chunk = ins[0].shape[0], 1024
    blocks = sum(len(ys) for _, ys in pairs)
    tot[...] = jnp.zeros((blocks * R, R), F32)

    def step(start):
        at, row = pl.ds(start, chunk), 0
        for x, ys in pairs:
            y = jnp.concatenate([ins[i][at, :] for i in ys], 1) if len(ys) > 1 else ins[ys[0]][at, :]
            d = lax.dot_general(ins[x][at, :], y, TN, preferred_element_type=F32)
            for n in range(len(ys)):
                tot[row : row + R, :] += d[:, n * R : n * R + R]
                row += R

    sweep(rows, chunk, step, 4 if blocks == 1 else 2)
    return blocks * R // 2


def sums_body(pairs, count, place, *refs):
    ins, (mine, give, tot) = refs[:count], refs[-3:]
    half = sums_into(pairs, ins, tot)
    c = place[0]
    mine[...] = tot[pl.ds(pl.multiple_of(c * half, 8), half), :]
    give[...] = tot[pl.ds(pl.multiple_of((1 - c) * half, 8), half), :]


def local_sums(place, pairs, arrays, after=()):
    blocks = sum(len(ys) for _, ys in pairs)
    half = blocks * R // 2
    return pl.pallas_call(
        functools.partial(sums_body, pairs, len(arrays)),
        out_shape=[jax.ShapeDtypeStruct((half, R), F32)] * 2,
        in_specs=[SMEM] + [VMEM] * len(arrays) + [ANY] * len(after),
        out_specs=[VMEM, VMEM],
        scratch_shapes=[pltpu.VMEM((blocks * R, R), F32)],
        cost_estimate=BRIEF,
        compiler_params=PARAMS,
        name="local_sums",
    )(place, *arrays, *after)


def over(block, axis, mask):
    return block + swap(block, axis, mask)


def over_chips(block):
    came = [swap(block, "front", mask) for mask in (2, 4, 6)]
    return (block + came[0]) + (came[1] + came[2])


def over_core(parts):
    mine, give = parts
    return mine + swap(give, "front", 1)


def factor_into(scale, place, sums, z_out, p_out, tot, m):
    c = place[0]
    late_from = 2 * R if len(sums) == 2 else 0
    for base, start, half, (mine, other) in (
        (0, 0, 2 * R, sums[:2]),
        (4 * R, late_from, R // 2, sums[-2:]),
    ):
        rows = slice(start, start + half)
        tot[pl.ds(pl.multiple_of(base + c * half, 8), half), :] = mine[rows, :]
        tot[pl.ds(pl.multiple_of(base + (1 - c) * half, 8), half), :] = other[rows, :]
    g11, b1, g22, b2, g12 = (tot[R * n : R * n + R, :] for n in range(5))
    bt = jnp.concatenate([b1, b2], 1)
    g = jnp.concatenate([jnp.concatenate([g11, g12], 1), jnp.concatenate([g12.T, g22], 1)], 0)
    bg = jnp.dot(bt, g, precision=HIGHEST, preferred_element_type=F32)
    m[:, 0:R] = lax.dot_general(bg, bt, NT, precision=HIGHEST, preferred_element_type=F32)
    m[:, R : 3 * R] = bt
    m[:, 3 * R : 5 * R] = bg
    panel, parts = 32, 5
    sub = lax.broadcasted_iota(jnp.int32, (8, R), 0)
    tiles = panel // 8

    def spread(x):
        return jnp.broadcast_to(x, (8, R))

    for top in range(0, R, panel):
        w = [
            [m[top + 8 * t : top + 8 * t + 8, R * q : R * q + R] for q in range(parts)]
            for t in range(tiles)
        ]
        for b in range(tiles):
            at = top + 8 * b
            v = {
                (i, t): spread(w[t][0][:, at + i : at + i + 1])
                for i in range(8)
                for t in range(b, tiles)
            }
            for i in range(8):
                inv = lax.rsqrt(spread(v[i, b][i : i + 1, :]))
                row = [spread(w[b][q][i : i + 1, :]) * inv for q in range(parts)]
                ahead = {j: spread(v[j, b][i : i + 1, :]) * inv for j in range(i + 1, 8)}
                for t in range(b, tiles):
                    mult = v[i, t] * inv
                    if t == b:
                        mult = jnp.where(sub > i, mult, 0.0)
                    for q in range(parts):
                        new = w[t][q] - mult * row[q]
                        w[t][q] = jnp.where(sub == i, row[q], new) if t == b else new
                    for j in range(i + 1, 8):
                        v[j, t] = v[j, t] - mult * ahead[j]
        u = jnp.concatenate([jnp.concatenate(r, 1) for r in w], 0)
        z_out[top : top + panel, :] = u[:, R : 3 * R] * scale
        p_out[top : top + panel, :] = u[:, 3 * R : 5 * R] * (1.0 / scale)
        if top + panel < R:
            update = lax.dot_general(u[:, 0:R], u, TN, precision=HIGHEST, preferred_element_type=F32)
            m[top + panel :, :] = m[top + panel :, :] - update[top + panel :, :]


FACTOR_SPACE = [
    pltpu.VMEM((R, 2 * R), F32),
    pltpu.VMEM((R, 2 * R), F32),
    pltpu.VMEM((5 * R, R), F32),
    pltpu.VMEM((R, 5 * R), F32),
]


def split(w):
    high = w.astype(BF16)
    return jnp.concatenate([high, (w - high.astype(F32)).astype(BF16)], 0)


def times(a, b, w):
    d = lax.dot_general(jnp.concatenate([a, b], 1), w, NT, preferred_element_type=F32)
    return (d[:, :R] + d[:, R:]).astype(BF16)


def left_body(scale, place, index, *refs):
    sums, (la_in, lb_in, left, lq, p_out, src, dst), refs = refs[:4], refs[4:11], refs[11:]
    space, (la, lb, sems) = refs[:4], refs[4:]
    copies = fetch((la_in, lb_in), (la, lb), sems)
    rows, chunk = la.shape[0], 512
    z, p = space[:2]
    factor_into(scale, place, sums, *space)
    p_out[...] = p[...]
    zz = split(z[...])
    for copy in copies:
        copy.wait()

    def step(start):
        at = pl.ds(start, chunk)
        new = times(la[at, :], lb[at, :], zz)
        left[at, :] = new
        src[at, :] = new.astype(F32)

    sweep(rows, chunk, step, 4)
    src[rows:, :] = jnp.zeros((8, R), F32)
    pick_rows(index, src, dst, (lq,), 1)


def new_left(scale, place, index, sums, la, lb):
    rows = la.shape[0]
    return pl.pallas_call(
        functools.partial(left_body, scale),
        out_shape=[jax.ShapeDtypeStruct((rows, R), BF16)] * 2
        + [jax.ShapeDtypeStruct((R, 2 * R), F32)],
        in_specs=[SMEM] * 2 + [VMEM] * 4 + [ANY] * 2,
        out_specs=[VMEM] * 3,
        scratch_shapes=gather_space(1, rows) + FACTOR_SPACE + held(rows, 2),
        cost_estimate=BRIEF,
        compiler_params=PARAMS,
        name="new_left",
    )(place, index, *sums, la, lb)


def rows_body(place, own, left, lq, la, mine, give, src, dst, tot):
    load_rows((left,), src)
    pick_rows(own, src, dst, (la,), 1)
    half = sums_into(((0, (0,)), (1, (1,))), (la, lq), tot)
    c = place[0]
    mine[...] = tot[pl.ds(pl.multiple_of(c * half, 8), half), :]
    give[...] = tot[pl.ds(pl.multiple_of((1 - c) * half, 8), half), :]


def left_rows(place, own, left, lq):
    rows = left.shape[0]
    return pl.pallas_call(
        rows_body,
        out_shape=[jax.ShapeDtypeStruct((rows, R), BF16)] + [jax.ShapeDtypeStruct((R, R), F32)] * 2,
        in_specs=[SMEM] * 2 + [VMEM] * 2,
        out_specs=[VMEM] * 3,
        scratch_shapes=gather_space(1, rows) + [pltpu.VMEM((2 * R, R), F32)],
        cost_estimate=BRIEF,
        compiler_params=PARAMS,
        name="left_rows",
    )(place, own, left, lq)


def right_body(top, place, own, asked, p, ra_in, rb_in, sk_in, sk_o_in, _, *refs):
    (ra_out, rq, mine, give, src, dst, tot), (ra, rb, sk, sk_o, sems) = refs[:7], refs[7:]
    copies = fetch((ra_in, rb_in, sk_in, sk_o_in), (ra, rb, sk, sk_o), sems)
    rows, chunk = ra.shape[0], 512
    pp = split(p[...])
    copies[0].wait()
    copies[1].wait()

    def step(start):
        at = pl.ds(start, chunk)
        src[at, :] = times(ra[at, :], rb[at, :], pp).astype(F32)

    sweep(rows, chunk, step, 4)
    src[rows:, :] = jnp.zeros((8, R), F32)
    pick_rows(own, src, dst, (ra_out,), 1)
    pick_rows(asked, src, dst, (rq,), 1)
    copies[2].wait()
    copies[3].wait()
    half = sums_into(((0, (1,)), (2, (3,))), (sk, ra_out, sk_o, rq), tot)
    c = place[0]
    mine[:half, :] = tot[pl.ds(pl.multiple_of(c * half, 8), half), :]
    give[:half, :] = tot[pl.ds(pl.multiple_of((1 - c) * half, 8), half), :]
    if top:
        for out, core in ((mine, c), (give, 1 - c)):
            rows_of = jnp.where(core == 0, ra_out[:R, :].astype(F32), rq[:R, :].astype(F32))
            out[half:, :] = jnp.where(place[1] == 1, rows_of, 0.0)


def right_rows(top, place, own, asked, p, ra, rb, sk, sk_o, after):
    rows = ra.shape[0]
    half = 2 * R if top else R
    return pl.pallas_call(
        functools.partial(right_body, top),
        out_shape=[jax.ShapeDtypeStruct((rows, R), BF16)] * 2
        + [jax.ShapeDtypeStruct((half, R), F32)] * 2,
        in_specs=[SMEM] * 3 + [VMEM] + [ANY] * 5,
        out_specs=[VMEM] * 4,
        scratch_shapes=gather_space(1, rows) + [pltpu.VMEM((2 * R, R), F32)] + held(rows, 4),
        cost_estimate=BRIEF,
        compiler_params=PARAMS,
        name="right_rows",
    )(place, own, asked, p, ra, rb, sk, sk_o, after)


def finish_body(scale, place, mine, other, top, top_o, pivot, *refs):
    sources, (left, right, panel), refs = refs[:5], refs[5:8], refs[8:]
    space, (la, lb, ra, rb, front, sems) = refs[:4], refs[4:]
    copies = fetch(sources, (la, lb, ra, rb, front), sems)
    rows, chunk = la.shape[0], 512
    z, p = space[:2]
    factor_into(scale, place, (mine, other), *space)
    zz, pp = split(z[...]), split(p[...])
    first = place[0] == 0
    tops = (top[...].astype(F32), top_o[...].astype(F32))
    right_piv = times(
        jnp.where(first, tops[0], tops[1]).astype(BF16),
        jnp.where(first, tops[1], tops[0]).astype(BF16),
        pp,
    )
    inverse = jnp.concatenate([pivot[...], pivot[...]], 0)
    for copy in copies:
        copy.wait()

    def step(start):
        at = pl.ds(start, chunk)
        new = times(la[at, :], lb[at, :], zz)
        left[at, :] = new
        right[at, :] = times(ra[at, :], rb[at, :], pp)
        updated = front[at, :].astype(F32) - lax.dot_general(
            new, right_piv, NT, preferred_element_type=F32
        )
        high = updated.astype(BF16)
        low = (updated - high.astype(F32)).astype(BF16)
        panel[at, :] = jnp.dot(
            jnp.concatenate([high, low], 1), inverse, preferred_element_type=F32
        ).astype(BF16)

    sweep(rows, chunk, step, 4)


def finish(scale, place, sums, tops, pivot, arrays):
    rows = arrays[0].shape[0]
    return pl.pallas_call(
        functools.partial(finish_body, scale),
        out_shape=[jax.ShapeDtypeStruct((rows, R), BF16)] * 3,
        in_specs=[SMEM] + [VMEM] * 5 + [ANY] * 5,
        out_specs=[VMEM] * 3,
        scratch_shapes=FACTOR_SPACE + held(rows, 5),
        cost_estimate=BRIEF,
        compiler_params=PARAMS,
        name="finish",
    )(place, *sums, *tops, pivot, *arrays)


def tied(array, *others):
    return lax.optimization_barrier((array, *others))[0]


def on_device(child_u, child_v, sketch, map_own, map_peer, live_rows, front_panel, pivot_inverse):
    rows, levels = child_u.shape[0], sketch.shape[0]
    fronts, front = lax.axis_size("front"), lax.axis_index("front")
    leaves = lax.axis_size("leaf")
    place = jnp.stack([front % 2, front == 0]).astype(jnp.int32)
    dead = jnp.arange(rows, dtype=jnp.int32)[None, :] >= live_rows
    own = jnp.where(dead, rows, map_own)
    peer = jnp.where(dead, rows, map_peer)
    near = swap(peer[:2], "leaf", 1)
    asked = [near[0], swap(near[1], "leaf", 3)]
    asked += [swap(peer[n], "leaf", 1 << n) for n in range(2, levels)]
    right_o = swap(child_v, "leaf", 1)
    sketch_o = [None, None] + [swap(sketch[n], "leaf", 1 << n) for n in range(2, levels)]
    (lq,) = gather(asked[0], child_u)
    lb = swap(lq, "leaf", 1)
    la, ra = gather(own[0], child_u, child_v)
    (rb,) = gather(peer[0], right_o)
    pairs = ((0, (0,)), (1, (2,)), (3, (3,)), (1, (4,)))
    early = over_core(local_sums(place, pairs, (la, sketch[0], ra, lq, rb), asked[1:]))
    for level in range(levels):
        bit, last = 1 << level, level == levels - 1
        scale = math.sqrt(2 * bit * fronts * rows)
        if level > 0:
            left, lq, p = new_left(scale_before, place, asked[level], sums, la, lb)
            lb = swap(lq, "leaf", bit)
            la, *gram = left_rows(place, own[level], left, lq)
            ra, rq, *cross = right_rows(
                last, place, own[level], asked[level], p, ra, rb, sketch[level], sketch_o[level], gram[0]
            )
            early = jnp.concatenate([over_core(gram), over_core(cross)], 0)
        early = over(early, "front", 2)
        after = (early,) if level else (early, *sketch_o[2:])
        late = over_core(local_sums(place, ((0, (1,)),), (la, lb), after))
        early = over(early, "front", 4)
        if last:
            break
        both = jnp.concatenate([early, late], 0)
        for b in range(level + 1):
            both = over(both, "leaf", 1 << b)
        if level == 0:
            sketch_o[1] = swap(tied(sketch[1], both), "leaf", 2)
        else:
            rb = swap(tied(rq, both), "leaf", bit)
        late = over_chips(both[2 * R :])
        sums = (both, swap(both, "front", 1), late, swap(late, "front", 1))
        scale_before = scale
    rb = swap(tied(rq, lb), "leaf", bit)
    across = [
        (n, n ^ (bit * fronts) if n % 2 else n) for n in range(leaves * fronts)
    ]
    top = lax.ppermute(early[2 * R :].astype(BF16), ("leaf", "front"), across)
    late = over_chips(late)
    both = jnp.concatenate([early[: 2 * R], late], 0)
    for b in range(level):
        both = over(both, "leaf", 1 << b)
    both = over(tied(both, rb, top), "leaf", bit)
    return finish(
        scale,
        place,
        (both, swap(both, "front", 1)),
        (top, swap(top, "front", 1)),
        pivot_inverse,
        (la, lb, ra, rb, front_panel),
    )


def solution(mesh):
    rows = P(("leaf", "front"), None)
    placed = (
        rows,
        rows,
        P(None, ("leaf", "front"), None),
        P(None, ("leaf", "front")),
        P(None, ("leaf", "front")),
        P(None, ("leaf", "front")),
        rows,
        P("leaf", None),
    )
    return jax.shard_map(
        on_device, mesh=mesh, in_specs=placed, out_specs=(rows, rows, rows), check_vma=False
    )
```

```python
import functools
import math

import jax
import jax.numpy as jnp
from jax import lax
from jax.experimental import pallas as pl
from jax.experimental.pallas import tpu as pltpu
from jax.sharding import PartitionSpec as P

F32, BF16 = jnp.float32, jnp.bfloat16
HIGHEST = lax.Precision.HIGHEST
NT = (((1,), (1,)), ((), ()))
TN = (((0,), (0,)), ((), ()))
VMEM = pl.BlockSpec(memory_space=pltpu.VMEM)
SMEM = pl.BlockSpec(memory_space=pltpu.SMEM)
ANY = pl.BlockSpec(memory_space=pl.ANY)
R = 128
HALF = 64
B1, B2, G11, G12, G22 = range(5)
ORDERS = ((G11, B1, G22, B2), (G12,)), ((G11, G22, B1), (G12, B2))
UNROLL = 32
BRIEF = pl.CostEstimate(flops=1, bytes_accessed=1, transcendentals=0)
PARAMS = pltpu.CompilerParams(vmem_limit_bytes=24 << 20)


def swap(block, axis, mask):
    route = [(i, i ^ mask) for i in range(lax.axis_size(axis))]
    return lax.ppermute(block, axis, route)


def fetch(sources, buffers, sems):
    copies = [
        pltpu.make_async_copy(source, buffer, sems.at[n])
        for n, (source, buffer) in enumerate(zip(sources, buffers))
    ]
    for copy in copies:
        copy.start()
    return copies


def held(rows, count):
    return [pltpu.VMEM((rows, R), BF16)] * count + [pltpu.SemaphoreType.DMA((count,))]


def sweep(rows, chunk, step, times=1):
    def body(k, carry):
        for n in range(times):
            step(pl.multiple_of(k * chunk * times + n * chunk, chunk))
        return carry

    lax.fori_loop(0, rows // (chunk * times), body, 0)


def load_rows(ins, src):
    rows, width, chunk = ins[0].shape[0], len(ins), 1024

    def step(at):
        for w in range(width):
            src[pl.ds(width * at + w, chunk, width), :] = ins[w][pl.ds(at, chunk), :].astype(F32)

    sweep(rows, chunk, step)
    src[width * rows :, :] = jnp.zeros((8, R), F32)


def copy_rows(index, src, dst, rows, width, count, skip):
    def step(g, carry):
        for k in range(UNROLL):
            j = g * UNROLL + k
            i = index[j]
            dst[pl.ds(pl.multiple_of(count * j, count), count), :] = src[
                pl.ds(pl.multiple_of(width * i, width) + skip, count), :
            ]
        return carry

    lax.fori_loop(0, rows // UNROLL, step, 0)


def pick_rows(index, src, dst, outs, width, skip=0):
    rows, count = outs[0].shape[0], len(outs)
    copy_rows(index, src, dst, rows, width, count, skip)

    def store(at):
        for w in range(count):
            outs[w][pl.ds(at, 1024), :] = dst[pl.ds(count * at + w, 1024, count), :].astype(BF16)

    sweep(rows, 1024, store)


def gather_body(width, index, *refs):
    ins, outs, src, dst = refs[:width], refs[width : 2 * width], refs[-2], refs[-1]
    load_rows(ins, src)
    pick_rows(index, src, dst, outs, width)


def gather_space(width, rows):
    return [pltpu.VMEM((width * rows + 8, R), F32), pltpu.VMEM((width * rows, R), F32)]


def gather(index, *arrays):
    rows, width = arrays[0].shape[0], len(arrays)
    return pl.pallas_call(
        functools.partial(gather_body, width),
        out_shape=[jax.ShapeDtypeStruct((rows, R), BF16)] * width,
        in_specs=[SMEM] + [VMEM] * width,
        out_specs=[VMEM] * width,
        scratch_shapes=gather_space(width, rows),
        cost_estimate=BRIEF,
        compiler_params=PARAMS,
        name="gather",
    )(index, *arrays)


def sums_into(pairs, ins, tot):
    rows, chunk = ins[0].shape[0], 1024
    blocks = sum(len(ys) for _, ys in pairs)
    tot[...] = jnp.zeros((blocks * R, R), F32)

    def step(start):
        at, row = pl.ds(start, chunk), 0
        for x, ys in pairs:
            y = jnp.concatenate([ins[i][at, :] for i in ys], 1) if len(ys) > 1 else ins[ys[0]][at, :]
            d = lax.dot_general(ins[x][at, :], y, TN, preferred_element_type=F32)
            for n in range(len(ys)):
                tot[row : row + R, :] += d[:, n * R : n * R + R]
                row += R

    sweep(rows, chunk, step, 4 // blocks)
    return blocks


def halves(tot, blocks, place, mine, give):
    for out, core in ((mine, place[0]), (give, 1 - place[0])):
        for n in range(blocks):
            at = pl.ds(pl.multiple_of(n * R + core * HALF, HALF), HALF)
            out[n * HALF : n * HALF + HALF, :] = tot[at, :]


def sums_body(pairs, count, place, *refs):
    ins, (mine, give, tot) = refs[:count], refs[-3:]
    halves(tot, sums_into(pairs, ins, tot), place, mine, give)


def local_sums(place, pairs, arrays, after=()):
    blocks = sum(len(ys) for _, ys in pairs)
    half = blocks * HALF
    return pl.pallas_call(
        functools.partial(sums_body, pairs, len(arrays)),
        out_shape=[jax.ShapeDtypeStruct((half, R), F32)] * 2,
        in_specs=[SMEM] + [VMEM] * len(arrays) + [ANY] * len(after),
        out_specs=[VMEM, VMEM],
        scratch_shapes=[pltpu.VMEM((blocks * R, R), F32)],
        cost_estimate=BRIEF,
        compiler_params=PARAMS,
        name="local_sums",
    )(place, *arrays, *after)


def over(block, axis, mask):
    return block + swap(block, axis, mask)


def over_chips(block):
    came = [swap(block, "front", mask) for mask in (2, 4, 6)]
    return (block + came[0]) + (came[1] + came[2])


def over_core(parts):
    mine, give = parts
    return mine + swap(give, "front", 1)


def factor_into(scale, orders, place, sums, z_out, p_out, tot, m):
    early, late = orders
    late_from = len(early) * HALF if len(sums) == 2 else 0
    for order, start, (mine, other) in ((early, 0, sums[:2]), (late, late_from, sums[-2:])):
        for n, block in enumerate(order):
            rows = slice(start + n * HALF, start + n * HALF + HALF)
            for core, ref in ((place[0], mine), (1 - place[0], other)):
                at = pl.ds(pl.multiple_of(block * R + core * HALF, HALF), HALF)
                tot[at, :] = ref[rows, :]
    b1, b2, g11, g12, g22 = (tot[R * n : R * n + R, :] for n in range(5))
    bt = jnp.concatenate([b1, b2], 1)
    g = jnp.concatenate([jnp.concatenate([g11, g12], 1), jnp.concatenate([g12.T, g22], 1)], 0)
    bg = jnp.dot(bt, g, precision=HIGHEST, preferred_element_type=F32)
    m[:, 0:R] = lax.dot_general(bg, bt, NT, precision=HIGHEST, preferred_element_type=F32)
    m[:, R : 3 * R] = bt
    m[:, 3 * R : 5 * R] = bg
    panel, parts = 32, 5
    sub = lax.broadcasted_iota(jnp.int32, (8, R), 0)
    tiles = panel // 8

    def spread(x):
        return jnp.broadcast_to(x, (8, R))

    for top in range(0, R, panel):
        w = [
            [m[top + 8 * t : top + 8 * t + 8, R * q : R * q + R] for q in range(parts)]
            for t in range(tiles)
        ]
        for b in range(tiles):
            at = top + 8 * b
            v = {
                (i, t): spread(w[t][0][:, at + i : at + i + 1])
                for i in range(8)
                for t in range(b, tiles)
            }
            for i in range(8):
                inv = lax.rsqrt(spread(v[i, b][i : i + 1, :]))
                row = [spread(w[b][q][i : i + 1, :]) * inv for q in range(parts)]
                ahead = {j: spread(v[j, b][i : i + 1, :]) * inv for j in range(i + 1, 8)}
                for t in range(b, tiles):
                    mult = v[i, t] * inv
                    if t == b:
                        mult = jnp.where(sub > i, mult, 0.0)
                    for q in range(parts):
                        new = w[t][q] - mult * row[q]
                        w[t][q] = jnp.where(sub == i, row[q], new) if t == b else new
                    for j in range(i + 1, 8):
                        v[j, t] = v[j, t] - mult * ahead[j]
        u = jnp.concatenate([jnp.concatenate(r, 1) for r in w], 0)
        z_out[top : top + panel, :] = u[:, R : 3 * R] * scale
        p_out[top : top + panel, :] = u[:, 3 * R : 5 * R] * (1.0 / scale)
        if top + panel < R:
            update = lax.dot_general(u[:, 0:R], u, TN, precision=HIGHEST, preferred_element_type=F32)
            m[top + panel :, :] = m[top + panel :, :] - update[top + panel :, :]


FACTOR_SPACE = [
    pltpu.VMEM((R, 2 * R), F32),
    pltpu.VMEM((R, 2 * R), F32),
    pltpu.VMEM((5 * R, R), F32),
    pltpu.VMEM((R, 5 * R), F32),
]


def split(w):
    high = w.astype(BF16)
    return jnp.concatenate([high, (w - high.astype(F32)).astype(BF16)], 0)


def times(a, b, w):
    d = lax.dot_general(jnp.concatenate([a, b], 1), w, NT, preferred_element_type=F32)
    return (d[:, :R] + d[:, R:]).astype(BF16)


def left_body(how, place, index, *refs):
    sums, (la_in, lb_in, left, lq, p_out, src, dst), refs = refs[:4], refs[4:11], refs[11:]
    space, (la, lb, sems) = refs[:4], refs[4:]
    copies = fetch((la_in, lb_in), (la, lb), sems)
    rows, chunk = la.shape[0], 512
    z, p = space[:2]
    factor_into(*how, place, sums, *space)
    p_out[...] = p[...]
    zz = split(z[...])
    for copy in copies:
        copy.wait()

    def step(start):
        at = pl.ds(start, chunk)
        new = times(la[at, :], lb[at, :], zz)
        left[at, :] = new
        src[at, :] = new.astype(F32)

    sweep(rows, chunk, step, 2)
    src[rows:, :] = jnp.zeros((8, R), F32)
    pick_rows(index, src, dst, (lq,), 1)


def new_left(how, place, index, sums, la, lb):
    rows = la.shape[0]
    return pl.pallas_call(
        functools.partial(left_body, how),
        out_shape=[jax.ShapeDtypeStruct((rows, R), BF16)] * 2
        + [jax.ShapeDtypeStruct((R, 2 * R), F32)],
        in_specs=[SMEM] * 2 + [VMEM] * 4 + [ANY] * 2,
        out_specs=[VMEM] * 3,
        scratch_shapes=gather_space(1, rows) + FACTOR_SPACE + held(rows, 2),
        cost_estimate=BRIEF,
        compiler_params=PARAMS,
        name="new_left",
    )(place, index, *sums, la, lb)


def rows_body(place, own, left, lq, la, mine, give, src, dst, tot):
    load_rows((left,), src)
    pick_rows(own, src, dst, (la,), 1)
    halves(tot, sums_into(((0, (0,)), (1, (1,))), (la, lq), tot), place, mine, give)


def left_rows(place, own, left, lq):
    rows = left.shape[0]
    return pl.pallas_call(
        rows_body,
        out_shape=[jax.ShapeDtypeStruct((rows, R), BF16)] + [jax.ShapeDtypeStruct((R, R), F32)] * 2,
        in_specs=[SMEM] * 2 + [VMEM] * 2,
        out_specs=[VMEM] * 3,
        scratch_shapes=gather_space(1, rows) + [pltpu.VMEM((2 * R, R), F32)],
        cost_estimate=BRIEF,
        compiler_params=PARAMS,
        name="left_rows",
    )(place, own, left, lq)


def right_body(top, place, own, asked, p, ra_in, rb_in, sk_in, _, __, *refs):
    (right, ra_out, mine, give, src, dst, tot), (ra, rb, sk, sems) = refs[:7], refs[7:]
    copies = fetch((ra_in, rb_in, sk_in), (ra, rb, sk), sems)
    rows, chunk = ra.shape[0], 512
    pp = split(p[...])
    copies[0].wait()
    copies[1].wait()

    def step(start):
        at = pl.ds(start, chunk)
        new = times(ra[at, :], rb[at, :], pp)
        right[at, :] = new
        src[at, :] = new.astype(F32)

    sweep(rows, chunk, step, 2)
    src[rows:, :] = jnp.zeros((8, R), F32)
    pick_rows(own, src, dst, (ra_out,), 1)
    copies[2].wait()
    halves(tot, sums_into(((0, (1,)),), (sk, ra_out), tot), place, mine, give)
    if top:
        copy_rows(asked, src, dst, R, 1, 1, 0)
        for out, core in ((mine, place[0]), (give, 1 - place[0])):
            rows_of = jnp.where(core == 0, ra_out[:R, :].astype(F32), dst[:R, :])
            out[HALF:, :] = jnp.where(place[1] == 1, rows_of, 0.0)


def right_rows(top, place, own, asked, p, ra, rb, sk, after):
    rows = ra.shape[0]
    half = HALF + (R if top else 0)
    return pl.pallas_call(
        functools.partial(right_body, top),
        out_shape=[jax.ShapeDtypeStruct((rows, R), BF16)] * 2
        + [jax.ShapeDtypeStruct((half, R), F32)] * 2,
        in_specs=[SMEM] * 3 + [VMEM] + [ANY] * 5,
        out_specs=[VMEM] * 4,
        scratch_shapes=gather_space(1, rows) + [pltpu.VMEM((R, R), F32)] + held(rows, 3),
        cost_estimate=BRIEF,
        compiler_params=PARAMS,
        name="right_rows",
    )(place, own, asked, p, ra, rb, sk, *after)


def finish_body(how, place, mine, other, top, top_o, pivot, *refs):
    sources, (left, right, panel), refs = refs[:5], refs[5:8], refs[8:]
    space, (la, lb, ra, rb, front, sems) = refs[:4], refs[4:]
    copies = fetch(sources, (la, lb, ra, rb, front), sems)
    rows, chunk = la.shape[0], 512
    z, p = space[:2]
    factor_into(*how, place, (mine, other), *space)
    zz, pp = split(z[...]), split(p[...])
    first = place[0] == 0
    tops = (top[...].astype(F32), top_o[...].astype(F32))
    right_piv = times(
        jnp.where(first, tops[0], tops[1]).astype(BF16),
        jnp.where(first, tops[1], tops[0]).astype(BF16),
        pp,
    )
    inverse = jnp.concatenate([pivot[...], pivot[...]], 0)
    for copy in copies:
        copy.wait()

    def step(start):
        at = pl.ds(start, chunk)
        new = times(la[at, :], lb[at, :], zz)
        left[at, :] = new
        right[at, :] = times(ra[at, :], rb[at, :], pp)
        updated = front[at, :].astype(F32) - lax.dot_general(
            new, right_piv, NT, preferred_element_type=F32
        )
        high = updated.astype(BF16)
        low = (updated - high.astype(F32)).astype(BF16)
        panel[at, :] = jnp.dot(
            jnp.concatenate([high, low], 1), inverse, preferred_element_type=F32
        ).astype(BF16)

    sweep(rows, chunk, step, 2)


def finish(how, place, sums, tops, pivot, arrays):
    rows = arrays[0].shape[0]
    return pl.pallas_call(
        functools.partial(finish_body, how),
        out_shape=[jax.ShapeDtypeStruct((rows, R), BF16)] * 3,
        in_specs=[SMEM] + [VMEM] * 5 + [ANY] * 5,
        out_specs=[VMEM] * 3,
        scratch_shapes=FACTOR_SPACE + held(rows, 5),
        cost_estimate=BRIEF,
        compiler_params=PARAMS,
        name="finish",
    )(place, *sums, *tops, pivot, *arrays)


def tied(array, *others):
    return lax.optimization_barrier((array, *others))[0]


def on_device(child_u, child_v, sketch, map_own, map_peer, live_rows, front_panel, pivot_inverse):
    rows, levels = child_u.shape[0], sketch.shape[0]
    fronts, front = lax.axis_size("front"), lax.axis_index("front")
    leaves = lax.axis_size("leaf")
    place = jnp.stack([front % 2, front == 0]).astype(jnp.int32)
    dead = jnp.arange(rows, dtype=jnp.int32)[None, :] >= live_rows
    own = jnp.where(dead, rows, map_own)
    peer = jnp.where(dead, rows, map_peer)
    near = swap(peer[:2], "leaf", 1)
    asked = [near[0], swap(near[1], "leaf", 3)]
    asked += [swap(peer[n], "leaf", 1 << n) for n in range(2, levels)]
    right_o = swap(child_v, "leaf", 1)
    sketch_o = [None, None] + [swap(sketch[n], "leaf", 1 << n) for n in range(2, levels)]
    (lq,) = gather(asked[0], child_u)
    lb = swap(lq, "leaf", 1)
    la, ra = gather(own[0], child_u, child_v)
    (rb,) = gather(peer[0], right_o)
    pairs = ((0, (0,)), (1, (2,)), (3, (3,)), (1, (4,)))
    early = over_core(local_sums(place, pairs, (la, sketch[0], ra, lq, rb), asked[1:]))
    for level in range(levels):
        bit, last = 1 << level, level == levels - 1
        how = (math.sqrt(2 * bit * fronts * rows), ORDERS[min(level, 1)])
        if level > 0:
            left, lq, p = new_left(how_before, place, asked[level], sums, la, lb)
            lb = swap(lq, "leaf", bit)
            la, *gram = left_rows(place, own[level], left, lq)
            right, ra, *cross = right_rows(
                last, place, own[level], asked[level], p, ra, rb, sketch[level], (gram[0], sketch_o[level])
            )
            early = jnp.concatenate([over_core(gram), over_core(cross)], 0)
            (rq,) = gather(asked[level], tied(right, early))
        early = over_chips(early)
        if level == 0:
            late = local_sums(place, ((0, (1,)),), (la, lb), (early, *sketch_o[2:]))
        else:
            pairs = ((0, (1,)), (2, (3,)))
            late = local_sums(place, pairs, (la, lb, sketch_o[level], rq), (early,))
        late = over_core(late)
        if last:
            break
        both = jnp.concatenate([early, late], 0)
        for b in range(level + 1):
            both = over(both, "leaf", 1 << b)
        if level == 0:
            sketch_o[1] = swap(tied(sketch[1], both), "leaf", 2)
        else:
            rb = swap(tied(rq, both), "leaf", bit)
        late = over_chips(both[early.shape[0] :])
        sums = (both, swap(both, "front", 1), late, swap(late, "front", 1))
        how_before = how
    rb = swap(tied(rq, lb), "leaf", bit)
    across = [
        (n, n ^ (bit * fronts) if n % 2 else n) for n in range(leaves * fronts)
    ]
    cut = early.shape[0] - R
    top = lax.ppermute(early[cut:].astype(BF16), ("leaf", "front"), across)
    late = over_chips(late)
    both = jnp.concatenate([early[:cut], late], 0)
    for b in range(level):
        both = over(both, "leaf", 1 << b)
    both = over(tied(both, rb, top), "leaf", bit)
    top_o = swap(top, "front", 1)
    return finish(
        how,
        place,
        (both, swap(tied(both, top_o), "front", 1)),
        (top, top_o),
        pivot_inverse,
        (la, lb, ra, rb, front_panel),
    )


def solution(mesh):
    rows = P(("leaf", "front"), None)
    placed = (
        rows,
        rows,
        P(None, ("leaf", "front"), None),
        P(None, ("leaf", "front")),
        P(None, ("leaf", "front")),
        P(None, ("leaf", "front")),
        rows,
        P("leaf", None),
    )
    return jax.shard_map(
        on_device, mesh=mesh, in_specs=placed, out_specs=(rows, rows, rows), check_vma=False
    )
```

```python
import functools
import math

import jax
import jax.numpy as jnp
from jax import lax
from jax.experimental import pallas as pl
from jax.experimental.pallas import tpu as pltpu
from jax.sharding import PartitionSpec as P

F32, BF16 = jnp.float32, jnp.bfloat16
HIGHEST = lax.Precision.HIGHEST
NT = (((1,), (1,)), ((), ()))
TN = (((0,), (0,)), ((), ()))
VMEM = pl.BlockSpec(memory_space=pltpu.VMEM)
SMEM = pl.BlockSpec(memory_space=pltpu.SMEM)
ANY = pl.BlockSpec(memory_space=pl.ANY)
R = 128
HALF = 64
B1, B2, G11, G12, G22 = range(5)
ORDERS = ((G11, B1, G22, B2), (G12,)), ((G11, G22, B1), (G12, B2))
UNROLL = 32
BRIEF = pl.CostEstimate(flops=1, bytes_accessed=1, transcendentals=0)
PARAMS = pltpu.CompilerParams(vmem_limit_bytes=24 << 20)


def swap(block, axis, mask):
    route = [(i, i ^ mask) for i in range(lax.axis_size(axis))]
    return lax.ppermute(block, axis, route)


def fetch(sources, buffers, sems):
    copies = [
        pltpu.make_async_copy(source, buffer, sems.at[n])
        for n, (source, buffer) in enumerate(zip(sources, buffers))
    ]
    for copy in copies:
        copy.start()
    return copies


def held(rows, count):
    return [pltpu.VMEM((rows, R), BF16)] * count + [pltpu.SemaphoreType.DMA((count,))]


def sweep(rows, chunk, step, times=1):
    def body(k, carry):
        for n in range(times):
            step(pl.multiple_of(k * chunk * times + n * chunk, chunk))
        return carry

    lax.fori_loop(0, rows // (chunk * times), body, 0)


def load_rows(ins, src):
    rows, width, chunk = ins[0].shape[0], len(ins), 512

    def step(at):
        for w in range(width):
            src[pl.ds(width * at + w, chunk, width), :] = ins[w][pl.ds(at, chunk), :].astype(F32)

    sweep(rows, chunk, step)
    src[width * rows :, :] = jnp.zeros((8, R), F32)


def copy_rows(index, src, dst, rows, width, count, skip):
    def step(g, carry):
        for k in range(UNROLL):
            j = g * UNROLL + k
            i = index[j]
            dst[pl.ds(pl.multiple_of(count * j, count), count), :] = src[
                pl.ds(pl.multiple_of(width * i, width) + skip, count), :
            ]
        return carry

    lax.fori_loop(0, rows // UNROLL, step, 0)


def pick_rows(index, src, dst, outs, width, skip=0):
    rows, count = outs[0].shape[0], len(outs)
    copy_rows(index, src, dst, rows, width, count, skip)

    def store(at):
        for w in range(count):
            outs[w][pl.ds(at, 512), :] = dst[pl.ds(count * at + w, 512, count), :].astype(BF16)

    sweep(rows, 512, store)


def gather_body(width, index, *refs):
    ins, outs, src, dst = refs[:width], refs[width : 2 * width], refs[-2], refs[-1]
    load_rows(ins, src)
    pick_rows(index, src, dst, outs, width)


def gather_space(width, rows):
    return [pltpu.VMEM((width * rows + 8, R), F32), pltpu.VMEM((width * rows, R), F32)]


def gather(index, *arrays):
    rows, width = arrays[0].shape[0], len(arrays)
    return pl.pallas_call(
        functools.partial(gather_body, width),
        out_shape=[jax.ShapeDtypeStruct((rows, R), BF16)] * width,
        in_specs=[SMEM] + [VMEM] * width,
        out_specs=[VMEM] * width,
        scratch_shapes=gather_space(width, rows),
        cost_estimate=BRIEF,
        compiler_params=PARAMS,
        name="gather",
    )(index, *arrays)


def sums_into(pairs, ins, tot):
    blocks = sum(len(ys) for _, ys in pairs)
    rows, chunk = ins[0].shape[0], 1024 if blocks < 4 else 512
    tot[...] = jnp.zeros((blocks * R, R), F32)

    def step(start):
        at, row = pl.ds(start, chunk), 0
        for x, ys in pairs:
            y = jnp.concatenate([ins[i][at, :] for i in ys], 1) if len(ys) > 1 else ins[ys[0]][at, :]
            d = lax.dot_general(ins[x][at, :], y, TN, preferred_element_type=F32)
            for n in range(len(ys)):
                tot[row : row + R, :] += d[:, n * R : n * R + R]
                row += R

    sweep(rows, chunk, step, 4 // blocks)
    return blocks


def halves(tot, blocks, place, mine, give):
    for out, core in ((mine, place[0]), (give, 1 - place[0])):
        for n in range(blocks):
            at = pl.ds(pl.multiple_of(n * R + core * HALF, HALF), HALF)
            out[n * HALF : n * HALF + HALF, :] = tot[at, :]


def sums_body(pairs, count, place, *refs):
    ins, (mine, give, tot) = refs[:count], refs[-3:]
    halves(tot, sums_into(pairs, ins, tot), place, mine, give)


def local_sums(place, pairs, arrays, after=()):
    blocks = sum(len(ys) for _, ys in pairs)
    half = blocks * HALF
    return pl.pallas_call(
        functools.partial(sums_body, pairs, len(arrays)),
        out_shape=[jax.ShapeDtypeStruct((half, R), F32)] * 2,
        in_specs=[SMEM] + [VMEM] * len(arrays) + [ANY] * len(after),
        out_specs=[VMEM, VMEM],
        scratch_shapes=[pltpu.VMEM((blocks * R, R), F32)],
        cost_estimate=BRIEF,
        compiler_params=PARAMS,
        name="local_sums",
    )(place, *arrays, *after)


def over(block, axis, mask):
    return block + swap(block, axis, mask)


def over_chips(block):
    came = [swap(block, "front", mask) for mask in (2, 4, 6)]
    return (block + came[0]) + (came[1] + came[2])


def over_leaves(block, level):
    if level == 0:
        return over(block, "leaf", 1)
    came = [swap(block, "leaf", mask) for mask in (1, 2, 3)]
    return (block + came[0]) + (came[1] + came[2])


def over_core(parts):
    mine, give = parts
    return mine + swap(give, "front", 1)


def factor_into(scale, orders, place, sums, z_out, p_out, tot, m):
    early, late = orders
    late_from = len(early) * HALF if len(sums) == 2 else 0
    for order, start, (mine, other) in ((early, 0, sums[:2]), (late, late_from, sums[-2:])):
        for n, block in enumerate(order):
            rows = slice(start + n * HALF, start + n * HALF + HALF)
            for core, ref in ((place[0], mine), (1 - place[0], other)):
                at = pl.ds(pl.multiple_of(block * R + core * HALF, HALF), HALF)
                tot[at, :] = ref[rows, :]
    b1, b2, g11, g12, g22 = (tot[R * n : R * n + R, :] for n in range(5))
    bt = jnp.concatenate([b1, b2], 1)
    g = jnp.concatenate([jnp.concatenate([g11, g12], 1), jnp.concatenate([g12.T, g22], 1)], 0)
    bg = jnp.dot(bt, g, precision=HIGHEST, preferred_element_type=F32)
    m[:, 0:R] = lax.dot_general(bg, bt, NT, precision=HIGHEST, preferred_element_type=F32)
    m[:, R : 3 * R] = bt
    m[:, 3 * R : 5 * R] = bg
    panel, parts = 32, 5
    sub = lax.broadcasted_iota(jnp.int32, (8, R), 0)
    tiles = panel // 8

    def spread(x):
        return jnp.broadcast_to(x, (8, R))

    for top in range(0, R, panel):
        w = [
            [m[top + 8 * t : top + 8 * t + 8, R * q : R * q + R] for q in range(parts)]
            for t in range(tiles)
        ]
        for b in range(tiles):
            at = top + 8 * b
            v = {
                (i, t): spread(w[t][0][:, at + i : at + i + 1])
                for i in range(8)
                for t in range(b, tiles)
            }
            for i in range(8):
                inv = lax.rsqrt(spread(v[i, b][i : i + 1, :]))
                row = [spread(w[b][q][i : i + 1, :]) * inv for q in range(parts)]
                ahead = {j: spread(v[j, b][i : i + 1, :]) * inv for j in range(i + 1, 8)}
                for t in range(b, tiles):
                    mult = v[i, t] * inv
                    if t == b:
                        mult = jnp.where(sub > i, mult, 0.0)
                    for q in range(parts):
                        new = w[t][q] - mult * row[q]
                        w[t][q] = jnp.where(sub == i, row[q], new) if t == b else new
                    for j in range(i + 1, 8):
                        v[j, t] = v[j, t] - mult * ahead[j]
        u = jnp.concatenate([jnp.concatenate(r, 1) for r in w], 0)
        z_out[top : top + panel, :] = u[:, R : 3 * R] * scale
        p_out[top : top + panel, :] = u[:, 3 * R : 5 * R] * (1.0 / scale)
        if top + panel < R:
            update = lax.dot_general(u[:, 0:R], u, TN, precision=HIGHEST, preferred_element_type=F32)
            m[top + panel :, :] = m[top + panel :, :] - update[top + panel :, :]


FACTOR_SPACE = [
    pltpu.VMEM((R, 2 * R), F32),
    pltpu.VMEM((R, 2 * R), F32),
    pltpu.VMEM((5 * R, R), F32),
    pltpu.VMEM((R, 5 * R), F32),
]


def split(w):
    high = w.astype(BF16)
    return jnp.concatenate([high, (w - high.astype(F32)).astype(BF16)], 0)


def times(a, b, w):
    d = lax.dot_general(jnp.concatenate([a, b], 1), w, NT, preferred_element_type=F32)
    return (d[:, :R] + d[:, R:]).astype(BF16)


def left_body(how, place, index, *refs):
    sums, (la_in, lb_in, left, lq, p_out, src, dst), refs = refs[:4], refs[4:11], refs[11:]
    space, (la, lb, sems) = refs[:4], refs[4:]
    copies = fetch((la_in, lb_in), (la, lb), sems)
    rows, chunk = la.shape[0], 512
    z, p = space[:2]
    factor_into(*how, place, sums, *space)
    p_out[...] = p[...]
    zz = split(z[...])
    for copy in copies:
        copy.wait()

    def step(start):
        at = pl.ds(start, chunk)
        new = times(la[at, :], lb[at, :], zz)
        left[at, :] = new
        src[at, :] = new.astype(F32)

    sweep(rows, chunk, step, 2)
    src[rows:, :] = jnp.zeros((8, R), F32)
    pick_rows(index, src, dst, (lq,), 1)


def new_left(how, place, index, sums, la, lb):
    rows = la.shape[0]
    return pl.pallas_call(
        functools.partial(left_body, how),
        out_shape=[jax.ShapeDtypeStruct((rows, R), BF16)] * 2
        + [jax.ShapeDtypeStruct((R, 2 * R), F32)],
        in_specs=[SMEM] * 2 + [VMEM] * 4 + [ANY] * 2,
        out_specs=[VMEM] * 3,
        scratch_shapes=gather_space(1, rows) + FACTOR_SPACE + held(rows, 2),
        cost_estimate=BRIEF,
        compiler_params=PARAMS,
        name="new_left",
    )(place, index, *sums, la, lb)


def rows_body(place, own, left, lq, la, mine, give, src, dst, tot):
    load_rows((left,), src)
    pick_rows(own, src, dst, (la,), 1)
    halves(tot, sums_into(((0, (0,)), (1, (1,))), (la, lq), tot), place, mine, give)


def left_rows(place, own, left, lq):
    rows = left.shape[0]
    return pl.pallas_call(
        rows_body,
        out_shape=[jax.ShapeDtypeStruct((rows, R), BF16)] + [jax.ShapeDtypeStruct((R, R), F32)] * 2,
        in_specs=[SMEM] * 2 + [VMEM] * 2,
        out_specs=[VMEM] * 3,
        scratch_shapes=gather_space(1, rows) + [pltpu.VMEM((2 * R, R), F32)],
        cost_estimate=BRIEF,
        compiler_params=PARAMS,
        name="left_rows",
    )(place, own, left, lq)


def right_body(top, place, own, asked, p, ra_in, rb_in, sk_in, _, __, *refs):
    (right, ra_out, mine, give, src, dst, tot), (ra, rb, sk, sems) = refs[:7], refs[7:]
    copies = fetch((ra_in, rb_in, sk_in), (ra, rb, sk), sems)
    rows, chunk = ra.shape[0], 512
    pp = split(p[...])
    copies[0].wait()
    copies[1].wait()

    def step(start):
        at = pl.ds(start, chunk)
        new = times(ra[at, :], rb[at, :], pp)
        right[at, :] = new
        src[at, :] = new.astype(F32)

    sweep(rows, chunk, step, 2)
    src[rows:, :] = jnp.zeros((8, R), F32)
    pick_rows(own, src, dst, (ra_out,), 1)
    copies[2].wait()
    halves(tot, sums_into(((0, (1,)),), (sk, ra_out), tot), place, mine, give)
    if top:
        copy_rows(asked, src, dst, R, 1, 1, 0)
        for out, core in ((mine, place[0]), (give, 1 - place[0])):
            rows_of = jnp.where(core == 0, ra_out[:R, :].astype(F32), dst[:R, :])
            out[HALF:, :] = jnp.where(place[1] == 1, rows_of, 0.0)


def right_rows(top, place, own, asked, p, ra, rb, sk, after):
    rows = ra.shape[0]
    half = HALF + (R if top else 0)
    return pl.pallas_call(
        functools.partial(right_body, top),
        out_shape=[jax.ShapeDtypeStruct((rows, R), BF16)] * 2
        + [jax.ShapeDtypeStruct((half, R), F32)] * 2,
        in_specs=[SMEM] * 3 + [VMEM] + [ANY] * 5,
        out_specs=[VMEM] * 4,
        scratch_shapes=gather_space(1, rows) + [pltpu.VMEM((R, R), F32)] + held(rows, 3),
        cost_estimate=BRIEF,
        compiler_params=PARAMS,
        name="right_rows",
    )(place, own, asked, p, ra, rb, sk, *after)


def finish_body(how, place, mine, other, top, top_o, pivot, *refs):
    sources, (left, right, panel), refs = refs[:5], refs[5:8], refs[8:]
    space, (la, lb, ra, rb, front, sems) = refs[:4], refs[4:]
    copies = fetch(sources, (la, lb, ra, rb, front), sems)
    rows, chunk = la.shape[0], 512
    z, p = space[:2]
    factor_into(*how, place, (mine, other), *space)
    zz, pp = split(z[...]), split(p[...])
    first = place[0] == 0
    tops = (top[...].astype(F32), top_o[...].astype(F32))
    right_piv = times(
        jnp.where(first, tops[0], tops[1]).astype(BF16),
        jnp.where(first, tops[1], tops[0]).astype(BF16),
        pp,
    )
    inverse = jnp.concatenate([pivot[...], pivot[...]], 0)
    for copy in copies:
        copy.wait()

    def step(start):
        at = pl.ds(start, chunk)
        new = times(la[at, :], lb[at, :], zz)
        left[at, :] = new
        right[at, :] = times(ra[at, :], rb[at, :], pp)
        updated = front[at, :].astype(F32) - lax.dot_general(
            new, right_piv, NT, preferred_element_type=F32
        )
        high = updated.astype(BF16)
        low = (updated - high.astype(F32)).astype(BF16)
        panel[at, :] = jnp.dot(
            jnp.concatenate([high, low], 1), inverse, preferred_element_type=F32
        ).astype(BF16)

    sweep(rows, chunk, step, 2)


def finish(how, place, sums, tops, pivot, arrays):
    rows = arrays[0].shape[0]
    return pl.pallas_call(
        functools.partial(finish_body, how),
        out_shape=[jax.ShapeDtypeStruct((rows, R), BF16)] * 3,
        in_specs=[SMEM] + [VMEM] * 5 + [ANY] * 5,
        out_specs=[VMEM] * 3,
        scratch_shapes=FACTOR_SPACE + held(rows, 5),
        cost_estimate=BRIEF,
        compiler_params=PARAMS,
        name="finish",
    )(place, *sums, *tops, pivot, *arrays)


def tied(array, *others):
    return lax.optimization_barrier((array, *others))[0]


def on_device(child_u, child_v, sketch, map_own, map_peer, live_rows, front_panel, pivot_inverse):
    rows, levels = child_u.shape[0], sketch.shape[0]
    fronts, front = lax.axis_size("front"), lax.axis_index("front")
    leaves = lax.axis_size("leaf")
    place = jnp.stack([front % 2, front == 0]).astype(jnp.int32)
    dead = jnp.arange(rows, dtype=jnp.int32)[None, :] >= live_rows
    own = jnp.where(dead, rows, map_own)
    peer = jnp.where(dead, rows, map_peer)
    near = swap(peer[:2], "leaf", 1)
    asked = [near[0], swap(near[1], "leaf", 3)]
    asked += [swap(peer[n], "leaf", 1 << n) for n in range(2, levels)]
    right_o = swap(child_v, "leaf", 1)
    sketch_o = [None, None] + [swap(sketch[n], "leaf", 1 << n) for n in range(2, levels)]
    (lq,) = gather(asked[0], child_u)
    lb = swap(lq, "leaf", 1)
    la, ra = gather(own[0], child_u, child_v)
    (rb,) = gather(peer[0], right_o)
    pairs = ((0, (0,)), (1, (2,)), (3, (3,)), (1, (4,)))
    early = over_core(local_sums(place, pairs, (la, sketch[0], ra, lq, rb), asked[1:]))
    for level in range(levels):
        bit, last = 1 << level, level == levels - 1
        how = (math.sqrt(2 * bit * fronts * rows), ORDERS[min(level, 1)])
        if level > 0:
            left, lq, p = new_left(how_before, place, asked[level], sums, la, lb)
            lb = swap(lq, "leaf", bit)
            la, *gram = left_rows(place, own[level], left, lq)
            right, ra, *cross = right_rows(
                last, place, own[level], asked[level], p, ra, rb, sketch[level], (gram[0], sketch_o[level])
            )
            early = jnp.concatenate([over_core(gram), over_core(cross)], 0)
            (rq,) = gather(asked[level], tied(right, early))
        early = over_chips(early)
        if level == 0:
            late = local_sums(place, ((0, (1,)),), (la, lb), (early, *sketch_o[2:]))
        else:
            pairs = ((0, (1,)), (2, (3,)))
            late = local_sums(place, pairs, (la, lb, sketch_o[level], rq), (early,))
        late = over_core(late)
        if last:
            break
        both = jnp.concatenate([early, late], 0)
        both = over_leaves(both, level)
        if level == 0:
            sketch_o[1] = swap(tied(sketch[1], both), "leaf", 2)
        else:
            rb = swap(tied(rq, both), "leaf", bit)
        late = over_chips(both[early.shape[0] :])
        sums = (both, swap(both, "front", 1), late, swap(late, "front", 1))
        how_before = how
    rb = swap(tied(rq, lb), "leaf", bit)
    across = [
        (n, n ^ (bit * fronts) if n % 2 else n) for n in range(leaves * fronts)
    ]
    cut = early.shape[0] - R
    top = lax.ppermute(early[cut:].astype(BF16), ("leaf", "front"), across)
    late = over_chips(late)
    both = jnp.concatenate([early[:cut], late], 0)
    both = over_leaves(both, level - 1)
    both = over(tied(both, rb, top), "leaf", bit)
    top_o = swap(top, "front", 1)
    return finish(
        how,
        place,
        (both, swap(tied(both, top_o), "front", 1)),
        (top, top_o),
        pivot_inverse,
        (la, lb, ra, rb, front_panel),
    )


def solution(mesh):
    rows = P(("leaf", "front"), None)
    placed = (
        rows,
        rows,
        P(None, ("leaf", "front"), None),
        P(None, ("leaf", "front")),
        P(None, ("leaf", "front")),
        P(None, ("leaf", "front")),
        rows,
        P("leaf", None),
    )
    return jax.shard_map(
        on_device, mesh=mesh, in_specs=placed, out_specs=(rows, rows, rows), check_vma=False
    )
```
